32 devices in a mesh: pipe: 4 (over y, x), expert: 8 (over z, core).
Axes of the slice: x: 2, y: 2, z: 4, core: 2. Of those that a mesh axis runs over, the one named last changes fastest.
Arguments:
- streams: bfloat16 [4, 2, 512, 3584], P('pipe', None, 'expert'), may hold values from -6 to 6
- norm_gain: float32 [4, 3584], P('pipe'), may hold values from 0.25 to 1.75
- w_gate: bfloat16 [4, 8, 3584, 512], P('pipe', 'expert'), may hold values from -0.09375 to 0.09375
- w_up: bfloat16 [4, 8, 3584, 512], P('pipe', 'expert'), may hold values from -0.09375 to 0.09375
- w_down: bfloat16 [4, 8, 512, 3584], P('pipe', 'expert'), may hold values from -0.1875 to 0.1875
- routes: int32 [4, 2, 512, 2], P('pipe', None, 'expert'), may hold values from 0 to 3, all different within a row; in each aligned block of 64 rows (0 to 63, 64 to 127, ..., all dimensions but the last counted through in order) at most 64 rows name the same one
- gate_weights: float32 [4, 2, 512, 2], P('pipe', None, 'expert'), may hold values from 0.2 to 1.2
Outputs:
- next_streams: bfloat16 [4, 2, 512, 3584], P('pipe', None, 'expert')
The draws below stay inside these ranges and needn't reach their ends.
Inputs may be any that keep to these rules, and one draw needn't show every extreme that they name: `routes`: each token names 2 different experts. Within each aligned block of 64 tokens of a micro-batch (the tokens of one device of the expert axis), at most 64 tokens name the same expert, a bound that some block reaches.
All inputs are finite; a program needn't handle non-finite values.
Results may differ from the reference program's by a relative error of at most 0.0051.
Values may be sent and summed in bfloat16 or wider, within the bound.
No kernel may reach another device: no remote copies, remote signals or barrier semaphores. Data moves between devices by JAX's collectives and lax.ppermute only.
A program may use at most 128 MiB of HBM per device.

```python
import math
import jax
import jax.numpy as jnp
import numpy as np
from jax import lax

D = 3584
FF = 1024
TOPK = 2
TOK_DEV = 64
EXPERTS = 4
TOKENS = 512
CAP = 64
N_PIPE = 4
N_EXPERT = 8


def block_levels(key, extent, split, smallest, high):
    def one(position, shards_of):
        draws = jax.random.uniform(jax.random.fold_in(jax.random.fold_in(key, 6), position), (shards_of,), jnp.float32, smallest / len(split), high / len(split))
        return jnp.repeat(jnp.exp(draws), extent[position] // shards_of).reshape((-1,) + (1,) * (len(extent) - position - 1))

    level = one(*split[0])
    for cut in split[1:]:
        level = level * one(*cut)
    return level


def assign_block(key, own, number, rows, number_of, top, bound, skew):
    order = jax.random.permutation(key, number_of)
    packed, ordinary = load_shares(number_of, rows * top, bound, skew, True), load_shares(number_of, rows * top, bound, skew, False)
    places = jnp.arange(number_of)

    def named(sizes, offset_by):
        used = int((sizes > 0).sum())
        fixed = max(1, used // 4)
        moved = fixed + (places - fixed + offset_by * (used - fixed)) % max(1, number_of - fixed)
        return jnp.zeros((number_of,), jnp.int32).at[order[jnp.where(places < fixed, places, moved)]].set(jnp.asarray(sizes, jnp.int32))

    sizes = jnp.where(number % 4 == 0, named(packed, number // 4), named(ordinary, number - number // 4 - 1))
    mixed = jax.random.permutation(jax.random.fold_in(own, 3), number_of)
    giver, sink = mixed[0:number_of // 2 * 2:2], mixed[1:number_of // 2 * 2:2]
    room = jnp.minimum(sizes[giver] - 1, bound - sizes[sink]) // 2
    room = jnp.where((giver == order[0]) | (sink == order[0]) | (sizes[sink] == 0), 0, jnp.maximum(room, 0))
    moved = jax.random.randint(jax.random.fold_in(own, 4), (number_of // 2,), 0, 1 << 20) % (room + 1)
    sizes = sizes.at[giver].add(-moved).at[sink].add(moved)
    members = jnp.searchsorted(jnp.cumsum(sizes), jnp.arange(rows * top), side="right").astype(jnp.int32)
    grid = members.reshape(top, rows).T
    grid = grid[jax.random.permutation(jax.random.fold_in(own, 1), rows)]
    offset_by = jax.random.randint(jax.random.fold_in(own, 2), (rows, 1), 0, top)
    return jnp.take_along_axis(grid, (jnp.arange(top)[None, :] + offset_by) % top, axis=1)


def load_shares(number_of, total, limit, slope, full):
    weights = [(1 << 20) // math.isqrt(standing ** slope) + 1 for standing in range(1, number_of + 1)]
    largest = limit if full else min(limit, max(-(-total // number_of), total * weights[0] // sum(weights)))
    least = 1 if total - largest >= number_of - 1 else 0
    given, rest = [largest] + [least] * (number_of - 1), total - largest - least * (number_of - 1)
    while rest > 0:
        movable = [i for i in range(1, number_of) if given[i] < largest] or [i for i in range(1, number_of) if given[i] < limit]
        pool, remaining = sum([weights[i] for i in movable]), rest
        for i in movable:
            extra = min(limit - given[i], max(1, remaining * weights[i] // pool), rest)
            given[i] = given[i] + extra
            rest = rest - extra
    return np.array(given)


def noise(own_key, extent, scale, most, cuts=(), held_as=jnp.bfloat16):
    level = block_levels(own_key, extent, cuts, -0.22, 0.18) if cuts else 1.0
    drawn = jax.random.normal(own_key, extent, jnp.float32) * scale * level
    return jnp.minimum(jnp.maximum(drawn, -most), most).astype(held_as)


def setup_inputs(seed: int = 0) -> dict:
    keys = jax.random.split(jax.random.key(seed), 8)
    streams = noise(keys[0], (N_PIPE, 2, TOKENS, D), 1.0, 6.0, ((0, 4), (2, 8)))
    norm_gain = jnp.clip(1.0 + 0.15 * jax.random.normal(keys[1], (N_PIPE, D), jnp.float32), 0.25, 1.75)
    w_gate = noise(keys[2], (N_PIPE, 2 * EXPERTS, D, FF // 2), D ** -0.5, 0.09375, ((0, 4), (1, 8)))
    w_up = noise(keys[3], (N_PIPE, 2 * EXPERTS, D, FF // 2), D ** -0.5, 0.09375, ((0, 4), (1, 8)))
    w_down = noise(keys[4], (N_PIPE, 2 * EXPERTS, FF // 2, D), FF ** -0.5, 0.1875, ((0, 4), (1, 8)))
    routes_keys = jax.random.split(jax.random.fold_in(keys[5], 1), N_PIPE * 2 * TOKENS // TOK_DEV)
    routes_turns = jax.random.permutation(jax.random.fold_in(keys[5], 3), N_PIPE * 2 * TOKENS // TOK_DEV)
    routes = jax.vmap(lambda own, number: assign_block(jax.random.fold_in(keys[5], 2), own, number, TOK_DEV, EXPERTS, TOPK, CAP, 2))(routes_keys, routes_turns).reshape((N_PIPE, 2, TOKENS, TOPK))
    gate_weights = jnp.clip(0.2 + 1 * jax.random.uniform(keys[6], (N_PIPE, 2, TOKENS, TOPK), jnp.float32) ** block_levels(keys[6], (N_PIPE, 2, TOKENS, TOPK), ((0, 4), (2, 8)), -0.2, 0.2), 0.2, 1.2)
    return dict(streams=streams, norm_gain=norm_gain, w_gate=w_gate, w_up=w_up, w_down=w_down, routes=routes, gate_weights=gate_weights)


def section_layer(operands):
    state_in, gain_row, gate_shard, up_shard, down_shard, chosen_all, weight_all = operands
    gate_full = gate_shard.reshape(EXPERTS, 2, D, FF // 2).transpose(0, 2, 1, 3).reshape(EXPERTS, D, FF)
    up_full = up_shard.reshape(EXPERTS, 2, D, FF // 2).transpose(0, 2, 1, 3).reshape(EXPERTS, D, FF)
    down_pair = down_shard.reshape(EXPERTS, 2, FF // 2, D)
    outputs = []
    for stream in range(2):
        state = state_in[stream].astype(jnp.float32)
        normed = (state * lax.rsqrt(lax.optimization_barrier(jnp.mean(state * state, axis=-1, keepdims=True)) + 1e-06) * gain_row).astype(jnp.bfloat16)
        blocks = chosen_all[stream].reshape(N_EXPERT, TOK_DEV * TOPK)
        onehot = (blocks[:, :, None] == jnp.arange(EXPERTS, dtype=jnp.int32)[None, None, :]).astype(jnp.int32)
        slot_rank = lax.optimization_barrier(jnp.sum((jnp.cumsum(onehot, axis=1) - onehot) * onehot, axis=-1)).astype(jnp.int32)
        column = (jnp.arange(N_EXPERT, dtype=jnp.int32)[:, None] * CAP + slot_rank).astype(jnp.int32)
        token_index = jnp.broadcast_to(jnp.arange(TOKENS, dtype=jnp.int32).reshape(N_EXPERT, TOK_DEV)[:, :, None], (N_EXPERT, TOK_DEV, TOPK)).reshape(N_EXPERT, TOK_DEV * TOPK)
        table = jnp.zeros((EXPERTS, N_EXPERT * CAP), jnp.int32).at[blocks, column].set(token_index)

        def one_expert(pieces):
            rows_of, gate_mat, up_mat, down_mats = pieces
            row_block = normed[rows_of]
            gate_val = jnp.dot(row_block, gate_mat, preferred_element_type=jnp.float32)
            up_val = jnp.dot(row_block, up_mat, preferred_element_type=jnp.float32)
            hidden = (jax.nn.silu(gate_val) * up_val).astype(jnp.bfloat16)
            first = jnp.dot(hidden[:, :FF // 2], down_mats[0], preferred_element_type=jnp.float32).astype(jnp.bfloat16)
            second = jnp.dot(hidden[:, FF // 2:], down_mats[1], preferred_element_type=jnp.float32).astype(jnp.bfloat16)
            return first.astype(jnp.float32) + second.astype(jnp.float32)
        expert_rows = lax.map(one_expert, (table, gate_full, up_full, down_pair))
        picked = expert_rows[blocks.reshape(-1), column.reshape(-1)].reshape(TOKENS, TOPK, D)
        mixed = state + lax.optimization_barrier(jnp.sum(weight_all[stream][:, :, None] * picked, axis=1))
        outputs.append(mixed.astype(jnp.bfloat16))
    return jnp.stack(outputs)

def reference(streams, norm_gain, w_gate, w_up, w_down, routes, gate_weights):
    layer_out = lax.map(section_layer, (streams, norm_gain, w_gate, w_up, w_down, routes, gate_weights))
    upward = jnp.roll(layer_out[:, 0], 1, axis=0)
    downward = jnp.roll(layer_out[:, 1], -1, axis=0)
    return jnp.stack([upward, downward], axis=1)
```

```python
import jax
import jax.numpy as jnp
from jax import lax
from jax.sharding import PartitionSpec as P

CHUNKS = 2


def swap_cores(value):
    count = lax.axis_size("expert")
    return lax.ppermute(value, "expert", [(i, i ^ 1) for i in range(count)])


def hop(value, up_from, down_from):
    pairs = [(2 * z, 2 * z + 2) for z in up_from] + [(2 * z + 1, 2 * z - 1) for z in down_from]
    return lax.ppermute(value, "expert", pairs)


def gather_hop(value, step):
    chips = lax.axis_size("expert") // 2
    return hop(value, range(step, chips - 1), range(1, chips - step))


def reduce_hop(value, step):
    chips = lax.axis_size("expert") // 2
    return hop(value, range(0, chips - 1 - step), range(1 + step, chips))


def ffn(rows, scale, gate_local, up_local, down_local):
    gate_val = jnp.dot(rows, gate_local, preferred_element_type=jnp.float32)
    up_val = jnp.dot(rows, up_local, preferred_element_type=jnp.float32)
    hidden = (jax.nn.silu(gate_val) * up_val * scale).astype(jnp.bfloat16)
    return jnp.dot(hidden, down_local, preferred_element_type=jnp.float32).astype(jnp.bfloat16)


def add(a, b):
    return (a.astype(jnp.float32) + b.astype(jnp.float32)).astype(jnp.bfloat16)


def chunk_pass(state, scale_of, weights):
    chips = lax.axis_size("expert") // 2
    rank = lax.axis_index("expert")
    chip, core = rank // 2, rank % 2
    rows = state.shape[0]
    normed = state
    own = jnp.concatenate([normed, swap_cores(normed)], axis=0)
    travelling = own
    partials = []
    for step in range(chips - 1):
        travelling = gather_hop(travelling, step)
        other = swap_cores(travelling)
        below, above = chip - 1 - step, chip + 1 + step
        if 2 * step <= chips - 3:
            first = jnp.where(core == 0, below, above)
            second = jnp.where(core == 0, above, below)
            given = ffn(travelling, scale_of(first, core), *weights)
            kept = ffn(other, scale_of(second, 1 - core), *weights)
            partials.append(add(kept, swap_cores(given)))
        else:
            from_below = below >= 0
            source_core = jnp.where(from_below, 0, 1)
            block = jnp.where(core == source_core, travelling, other)
            half = ffn(block, scale_of(jnp.where(from_below, below, above), source_core), *weights)
            partials.append(add(half, swap_cores(half)))
    local = ffn(own, scale_of(chip, core), *weights)
    total = None
    for step in reversed(range(chips - 1)):
        payload = partials[step] if total is None else add(partials[step], total)
        total = reduce_hop(payload, step)
    given = add(total[:rows], local[rows:])
    return total[rows:].astype(jnp.float32) + local[:rows].astype(jnp.float32) + swap_cores(given).astype(jnp.float32)


def body(streams, norm_gain, w_gate, w_up, w_down, routes, gate_weights):
    chips = lax.axis_size("expert") // 2
    sections = lax.axis_size("pipe")
    weights = (w_gate[0, 0], w_up[0, 0], w_down[0, 0])
    tokens = streams.shape[2]
    per_stream = CHUNKS // 2
    rows = tokens // per_stream
    named = routes[0][..., None] == jnp.arange(chips, dtype=jnp.int32)
    dense = jnp.sum(jnp.where(named, gate_weights[0][..., None], 0.0), axis=2)
    dense_all = lax.all_gather(dense, "expert").reshape(chips, 2, 2, tokens, chips)
    mine = jnp.sum(jnp.where(jnp.arange(chips) == lax.axis_index("expert") // 2, dense_all, 0.0), axis=-1)
    outs = []
    for stream in range(2):
        state = streams[0, stream].astype(jnp.float32)
        normed = (
            state * lax.rsqrt(jnp.mean(state * state, axis=-1, keepdims=True) + 1e-06) * norm_gain[0]
        ).astype(jnp.bfloat16)
        pieces = []
        for part in range(per_stream):
            cut = slice(part * rows, (part + 1) * rows)

            def scale_of(chip, first_core, stream=stream, cut=cut):
                block = lax.dynamic_index_in_dim(mine[:, :, stream, cut], jnp.clip(chip, 0, chips - 1), 0, keepdims=False)
                block = jnp.where(first_core == 0, block, block[::-1])
                return block.reshape(-1, 1)

            mixed = state[cut] + chunk_pass(normed[cut], scale_of, weights)
            shift = 1 if stream == 0 else sections - 1
            pairs = [(source, (source + shift) % sections) for source in range(sections)]
            pieces.append(lax.ppermute(mixed.astype(jnp.bfloat16), "pipe", pairs))
        outs.append(jnp.concatenate(pieces, axis=0))
    return jnp.stack(outs)[None]


def solution(mesh):
    return jax.shard_map(
        body,
        mesh=mesh,
        in_specs=(
            P("pipe", None, "expert", None),
            P("pipe", None),
            P("pipe", "expert", None, None),
            P("pipe", "expert", None, None),
            P("pipe", "expert", None, None),
            P("pipe", None, "expert", None),
            P("pipe", None, "expert", None),
        ),
        out_specs=P("pipe", None, "expert", None),
        check_vma=False,
    )
```

```python
import functools

import jax
import jax.numpy as jnp
from jax import lax
from jax.experimental import pallas as pl
from jax.experimental.pallas import tpu as pltpu
from jax.sharding import PartitionSpec as P

PARTS = 2
TAIL = 128
NO_COST = pl.CostEstimate(flops=1024, bytes_accessed=1024, transcendentals=0)
NEAR = pl.BlockSpec(memory_space=pltpu.VMEM)
ANYWHERE = pl.BlockSpec(memory_space=pl.ANY)
LIMIT = pltpu.CompilerParams(vmem_limit_bytes=16 << 20)


def swap_cores(value):
    count = lax.axis_size("expert")
    return lax.ppermute(value, "expert", [(i, i ^ 1) for i in range(count)])


def hop_pairs(step):
    chips = lax.axis_size("expert") // 2
    up = [(2 * z, 2 * z + 2) for z in range(step, chips - 1)]
    down = [(2 * z + 1, 2 * z - 1) for z in range(1, chips - step)]
    return up + down


def gather_hop(value, step):
    return lax.ppermute(value, "expert", hop_pairs(step))


def reduce_hop(value, step):
    return lax.ppermute(value, "expert", [(target, source) for source, target in hop_pairs(step)])


def near(*values):
    return [pltpu.with_memory_space_constraint(x, pltpu.VMEM) for x in values]


class Order:
    def __init__(self):
        self.before = []

    def call(self, kernel, out_shape, in_specs, operands, out_specs=NEAR, **options):
        before, count = self.before, len(operands)
        result = pl.pallas_call(
            lambda *refs: kernel(*refs[:count], *refs[count + len(before):]),
            out_shape=out_shape,
            in_specs=in_specs + [ANYWHERE] * len(before),
            out_specs=jax.tree.map(lambda _: out_specs, out_shape),
            compiler_params=LIMIT,
            cost_estimate=NO_COST,
            **options,
        )(*operands, *before)
        self.before = [jax.tree.leaves(result)[0]]
        return result

    def wait(self, value):
        return self.call(
            lambda here, out: None,
            jax.ShapeDtypeStruct(value.shape, value.dtype),
            [ANYWHERE],
            [value],
            out_specs=ANYWHERE,
            input_output_aliases={0: 0},
            name="arrived",
        )


def load_kernel(*refs):
    *pairs, sems = refs
    half = len(pairs) // 2
    copies = [pltpu.make_async_copy(pairs[k], pairs[half + k], sems.at[k]) for k in range(half)]
    for copy in copies:
        copy.start()
    for copy in copies:
        copy.wait()


def ffn_kernel(count, *refs):
    blocks, (mask, gate_a, up_a, down_a, gate_b, up_b, down_b), outs = refs[:count], refs[count:count + 7], refs[count + 7:]
    width = gate_a.shape[0]
    half = width // 2
    block = jnp.concatenate([b[...] for b in blocks], axis=0)
    rows = block[:, :width]
    scale = jnp.sum(block[:, width:].astype(jnp.float32) * mask[...], axis=-1, keepdims=True)

    def hidden(gate_w, up_w):
        gate_val = jnp.dot(rows, gate_w[...], preferred_element_type=jnp.float32)
        up_val = jnp.dot(rows, up_w[...], preferred_element_type=jnp.float32)
        return (gate_val / (1.0 + jnp.exp(-gate_val)) * up_val * scale).astype(jnp.bfloat16)

    first, second = hidden(gate_a, up_a), hidden(gate_b, up_b)
    for k in range(2):
        part = pl.ds(k * half, half)
        result = jnp.dot(first, down_a[:, part], preferred_element_type=jnp.float32)
        result += jnp.dot(second, down_b[:, part], preferred_element_type=jnp.float32)
        result = result.astype(jnp.bfloat16)
        start = 0
        for out in outs:
            out[:, part] = result[start:start + out.shape[0]]
            start += out.shape[0]


def sum_kernel(starts, *refs):
    *terms, out = refs
    rows = out.shape[0]
    total = terms[0][pl.ds(starts[0], rows)].astype(jnp.float32)
    for term, start in zip(terms[1:], starts[1:]):
        total += term[pl.ds(start, rows)].astype(jnp.float32)
    out[...] = total.astype(jnp.bfloat16)


def stack_kernel(*refs):
    *parts, out = refs
    start = 0
    for part in parts:
        out[pl.ds(start, part.shape[0])] = part[...]
        start += part.shape[0]


class Device:
    def __init__(self, order, weights, mask):
        self.order, self.weights, self.mask = order, weights, mask

    def load(self):
        own = self.order.call(
            load_kernel,
            [pltpu.VMEM(w.shape, w.dtype) for w in self.weights],
            [ANYWHERE] * len(self.weights),
            [pltpu.with_memory_space_constraint(w, pltpu.HBM) for w in self.weights],
            scratch_shapes=[pltpu.SemaphoreType.DMA((len(self.weights),))],
            name="weights_to_vmem",
        )
        self.weights = (*own, *(swap_cores(w) for w in own))

    def ffn(self, blocks, parts):
        rows = sum(block.shape[0] for block in blocks) // parts
        return self.order.call(
            functools.partial(ffn_kernel, len(blocks)),
            [jax.ShapeDtypeStruct((rows, self.weights[0].shape[0]), jnp.bfloat16)] * parts,
            [NEAR] * (len(blocks) + 7),
            near(*blocks, self.mask, *self.weights),
            name="expert",
        )

    def add(self, *terms, rows=None):
        terms = [term if isinstance(term, tuple) else (term, 0) for term in terms]
        rows = rows or terms[0][0].shape[0]
        return self.order.call(
            functools.partial(sum_kernel, [start for _, start in terms]),
            jax.ShapeDtypeStruct((rows, terms[0][0].shape[1]), jnp.bfloat16),
            [NEAR] * len(terms),
            near(*[term for term, _ in terms]),
            name="sum",
        )

    def stack(self, *parts):
        rows = sum(part.shape[0] for part in parts)
        return self.order.call(
            stack_kernel,
            jax.ShapeDtypeStruct((rows, parts[0].shape[1]), jnp.bfloat16),
            [NEAR] * len(parts),
            near(*parts),
            name="stack",
        )


class Chunk:
    def __init__(self, device, own, state, local, pairs, together):
        self.device, self.own, self.state, self.local, self.pairs = device, own, state, local, pairs
        self.last = lax.axis_size("expert") // 2 - 2
        self.rows = own[0].shape[0] // 2
        self.together = together
        self.moving, self.held, self.partials, self.shifted = {}, [], [], []

    def depart(self, after=True):
        for part, own in enumerate(self.own):
            self.moving[part] = gather_hop(self.device.order.wait(own) if after else own, 0)

    def gather(self, step):
        blocks = []
        for part in range(len(self.own)):
            blocks.append(self.device.order.wait(self.moving[part]))
            if step < self.last:
                self.moving[part] = gather_hop(blocks[part], step + 1)
        self.held.append(blocks)

    def work(self):
        for blocks in self.held:
            self.partials.append(self.device.ffn(blocks, 1 if self.together else len(blocks)))
        self.held = []

    def send_back(self):
        self.sums = [reduce_hop(partial, self.last) for partial in self.partials[self.last]]

    def go_on(self, step):
        for part, value in enumerate(self.sums):
            total = self.device.add(self.partials[step][part], self.device.order.wait(value))
            self.sums[part] = reduce_hop(total, step)

    def finish(self):
        rows = self.rows
        start = 0
        for value in self.sums:
            total = self.device.order.wait(value)
            cuts = range(0, total.shape[0], 2 * rows)
            theirs = swap_cores(jnp.concatenate([total[c + rows:c + 2 * rows] for c in cuts], axis=0))
            mine = jnp.concatenate([total[c:c + rows] for c in cuts], axis=0)
            state = self.state[start:start + mine.shape[0]]
            mixed = self.device.add(state, (self.local[0], self.local[1] + start), mine, theirs)
            self.shifted.append(lax.ppermute(mixed, "pipe", self.pairs))
            start += mine.shape[0]

    def settle(self):
        self.shifted = [self.device.order.wait(value) for value in self.shifted]

    def result(self):
        return jnp.concatenate(self.shifted, axis=0)


def in_parts(value):
    parts = []
    for _ in range(3):
        parts.append(value.astype(jnp.bfloat16))
        value = value - parts[-1].astype(jnp.float32)
    return parts


def body(streams, norm_gain, w_gate, w_up, w_down, routes, gate_weights):
    chips = lax.axis_size("expert") // 2
    sections = lax.axis_size("pipe")
    weights = (w_gate[0, 0], w_up[0, 0], w_down[0, 0])
    tokens = streams.shape[2]
    rows = tokens // PARTS
    named = routes[0][..., None] == jnp.arange(chips, dtype=jnp.int32)
    dense = jnp.sum(jnp.where(named, gate_weights[0][..., None], 0.0), axis=2)
    tail = jnp.concatenate(in_parts(dense), axis=-1)
    tail = jnp.pad(tail, ((0, 0), (0, 0), (0, TAIL - tail.shape[-1])))
    lane = jnp.arange(TAIL)
    mask = ((lane % chips == lax.axis_index("expert") // 2) & (lane < 3 * chips)).astype(jnp.float32)[None]
    wide = streams[0].astype(jnp.float32)
    normed = (
        wide * lax.rsqrt(jnp.mean(wide * wide, axis=-1, keepdims=True) + 1e-06) * norm_gain[0]
    ).astype(jnp.bfloat16)
    sent, mask = lax.optimization_barrier((jnp.concatenate([normed, tail], axis=-1), mask))
    swapped = swap_cores(sent)
    device = Device(Order(), weights, mask)
    own = [
        [device.stack(sent[stream, cut:cut + rows], swapped[stream, cut:cut + rows]) for cut in range(0, tokens, rows)]
        for stream in range(2)
    ]
    chunks = []
    local = []
    for stream in range(2):
        step = 1 if stream == 0 else sections - 1
        pairs = [(source, (source + step) % sections) for source in range(sections)]
        chunks.append(Chunk(device, own[stream], streams[0, stream], None, pairs, together=stream == 0))
    one, two = chunks
    last = one.last
    one.depart(after=False)
    device.load()
    for step in range(last):
        one.gather(step)
    two.depart()
    one.work()
    one.gather(last)
    one.work()
    one.send_back()
    for step in range(last):
        two.gather(step)
        two.work()
        if step == 0:
            (local,) = device.ffn([sent.reshape(-1, sent.shape[-1])], 1)
            one.local, two.local = (local, 0), (local, tokens)
        if step < last - 1 or last == 1:
            one.go_on(last - 1 - step)
    two.gather(last)
    two.work()
    two.send_back()
    one.go_on(0)
    for step in reversed(range(1, last)):
        two.go_on(step)
    one.finish()
    two.go_on(0)
    one.settle()
    two.finish()
    return jnp.stack([one.result(), two.result()])[None]


def solution(mesh):
    return jax.shard_map(
        body,
        mesh=mesh,
        in_specs=(
            P("pipe", None, "expert", None),
            P("pipe", None),
            P("pipe", "expert", None, None),
            P("pipe", "expert", None, None),
            P("pipe", "expert", None, None),
            P("pipe", None, "expert", None),
            P("pipe", None, "expert", None),
        ),
        out_specs=P("pipe", None, "expert", None),
        check_vma=False,
    )
```

```python
import functools

import jax
import jax.numpy as jnp
from jax import lax
from jax.experimental import pallas as pl
from jax.experimental.pallas import tpu as pltpu
from jax.sharding import PartitionSpec as P

PARTS = 2
TAIL = 128
NO_COST = pl.CostEstimate(flops=1024, bytes_accessed=1024, transcendentals=0)
NEAR = pl.BlockSpec(memory_space=pltpu.VMEM)
ANYWHERE = pl.BlockSpec(memory_space=pl.ANY)
LIMIT = pltpu.CompilerParams(vmem_limit_bytes=16 << 20)


def swap_cores(value):
    count = lax.axis_size("expert")
    return lax.ppermute(value, "expert", [(i, i ^ 1) for i in range(count)])


def hop_pairs(step):
    chips = lax.axis_size("expert") // 2
    up = [(2 * z, 2 * z + 2) for z in range(step, chips - 1)]
    down = [(2 * z + 1, 2 * z - 1) for z in range(1, chips - step)]
    return up + down


def gather_hop(value, step):
    return lax.ppermute(value, "expert", hop_pairs(step))


def reduce_hop(value, step):
    return lax.ppermute(value, "expert", [(target, source) for source, target in hop_pairs(step)])


def near(*values):
    return [pltpu.with_memory_space_constraint(x, pltpu.VMEM) for x in values]


class Order:
    def __init__(self, first):
        self.before = [first]

    def call(self, kernel, out_shape, in_specs, operands, out_specs=NEAR, **options):
        before, count = self.before, len(operands)
        result = pl.pallas_call(
            lambda *refs: kernel(*refs[:count], *refs[count + len(before):]),
            out_shape=out_shape,
            in_specs=in_specs + [ANYWHERE] * len(before),
            out_specs=jax.tree.map(lambda _: out_specs, out_shape),
            **{"compiler_params": LIMIT, "cost_estimate": NO_COST, **options},
        )(*operands, *before)
        self.before = [jax.tree.leaves(result)[0]]
        return result

    def wait(self, value):
        return self.call(
            lambda here, out: None,
            jax.ShapeDtypeStruct(value.shape, value.dtype),
            [ANYWHERE],
            [value],
            out_specs=ANYWHERE,
            input_output_aliases={0: 0},
            name="arrived",
        )


def begin_kernel(chips, *refs):
    sources, out, weights, copied, sems = refs[:7], refs[7], refs[8:11], refs[11:15], refs[15]
    copies = [pltpu.make_async_copy(a, b, sems.at[k]) for k, (a, b) in enumerate(zip(sources, (*copied, *weights)))]
    for copy in copies:
        copy.start()
    for copy in copies[:4]:
        copy.wait()
    streams, gain, routes, gates = copied
    _, tokens, width = streams.shape
    square = (tokens, tokens)
    diagonal = lax.broadcasted_iota(jnp.int32, square, 0) == lax.broadcasted_iota(jnp.int32, square, 1)
    lane = lax.broadcasted_iota(jnp.int32, (tokens, TAIL), 1)
    expert, addend = jnp.full((tokens, TAIL), -1, jnp.int32), jnp.zeros((tokens, TAIL), jnp.int32)
    for which in range(3):
        for e in range(chips):
            here = lane == which * chips + e
            expert, addend = jnp.where(here, e, expert), jnp.where(here, which, addend)

    def column(row):
        return jnp.sum(jnp.where(diagonal, row, 0), axis=1, keepdims=True)

    for stream in range(streams.shape[0]):
        place = pl.ds(stream * tokens, tokens)
        state = streams[stream].astype(jnp.float32)
        scale = lax.rsqrt(jnp.mean(state * state, axis=-1, keepdims=True) + 1e-06)
        out[place, pl.ds(0, width)] = (state * scale * gain[...]).astype(jnp.bfloat16)
        left = jnp.zeros((tokens, TAIL), jnp.float32)
        for k in range(routes.shape[1]):
            named = column(routes[stream, pl.ds(k, 1)]) == expert
            left += jnp.where(named, column(gates[stream, pl.ds(k, 1)]), 0.0)
        tail = jnp.zeros((tokens, TAIL), jnp.float32)
        for which in range(3):
            rounded = left.astype(jnp.bfloat16).astype(jnp.float32)
            tail = jnp.where(addend == which, rounded, tail)
            left = left - rounded
        out[place, pl.ds(width, TAIL)] = tail.astype(jnp.bfloat16)
    for copy in copies[4:]:
        copy.wait()


def norm_kernel(chips, *refs):
    sources, outs, copied, sems = refs[:4], refs[4:-5], refs[-5:-1], refs[-1]
    copies = [pltpu.make_async_copy(a, b, sems.at[k]) for k, (a, b) in enumerate(zip(sources, copied))]
    for copy in copies:
        copy.start()
    for copy in copies:
        copy.wait()
    streams, gain, routes, gates = copied
    _, tokens, width = streams.shape
    square = (tokens, tokens)
    diagonal = lax.broadcasted_iota(jnp.int32, square, 0) == lax.broadcasted_iota(jnp.int32, square, 1)
    lane = lax.broadcasted_iota(jnp.int32, (tokens, TAIL), 1)
    expert, addend = jnp.full((tokens, TAIL), -1, jnp.int32), jnp.zeros((tokens, TAIL), jnp.int32)
    for which in range(3):
        for e in range(chips):
            here = lane == which * chips + e
            expert, addend = jnp.where(here, e, expert), jnp.where(here, which, addend)

    def column(row):
        return jnp.sum(jnp.where(diagonal, row, 0), axis=1, keepdims=True)

    for stream in range(streams.shape[0]):
        place = pl.ds(stream * tokens, tokens)
        state = streams[stream].astype(jnp.float32)
        scale = lax.rsqrt(jnp.mean(state * state, axis=-1, keepdims=True) + 1e-06)
        out[place, pl.ds(0, width)] = (state * scale * gain[...]).astype(jnp.bfloat16)
        left = jnp.zeros((tokens, TAIL), jnp.float32)
        for k in range(routes.shape[1]):
            named = column(routes[stream, pl.ds(k, 1)]) == expert
            left += jnp.where(named, column(gates[stream, pl.ds(k, 1)]), 0.0)
        tail = jnp.zeros((tokens, TAIL), jnp.float32)
        for which in range(3):
            rounded = left.astype(jnp.bfloat16).astype(jnp.float32)
            tail = jnp.where(addend == which, rounded, tail)
            left = left - rounded
        out[place, pl.ds(width, TAIL)] = tail.astype(jnp.bfloat16)
    for copy in copies[4:]:
        copy.wait()


def load_kernel(*refs):
    *pairs, sems = refs
    half = len(pairs) // 2
    copies = [pltpu.make_async_copy(pairs[k], pairs[half + k], sems.at[k]) for k in range(half)]
    for copy in copies:
        copy.start()
    for copy in copies:
        copy.wait()


def ffn_kernel(count, *refs):
    blocks, (mask, gate_a, up_a, down_a, gate_b, up_b, down_b), outs = refs[:count], refs[count:count + 7], refs[count + 7:]
    width = gate_a.shape[0]
    half = width // 2
    block = jnp.concatenate([b[...] for b in blocks], axis=0)
    rows = block[:, :width]
    scale = jnp.sum(block[:, width:].astype(jnp.float32) * mask[...], axis=-1, keepdims=True)

    def hidden(gate_w, up_w):
        gate_val = jnp.dot(rows, gate_w[...], preferred_element_type=jnp.float32)
        up_val = jnp.dot(rows, up_w[...], preferred_element_type=jnp.float32)
        return (gate_val / (1.0 + jnp.exp(-gate_val)) * up_val * scale).astype(jnp.bfloat16)

    first, second = hidden(gate_a, up_a), hidden(gate_b, up_b)
    for k in range(2):
        part = pl.ds(k * half, half)
        result = jnp.dot(first, down_a[:, part], preferred_element_type=jnp.float32)
        result += jnp.dot(second, down_b[:, part], preferred_element_type=jnp.float32)
        result = result.astype(jnp.bfloat16)
        start = 0
        for out in outs:
            out[:, part] = result[start:start + out.shape[0]]
            start += out.shape[0]


def sum_kernel(starts, *refs):
    *terms, out = refs
    rows = out.shape[0]
    total = terms[0][pl.ds(starts[0], rows)].astype(jnp.float32)
    for term, start in zip(terms[1:], starts[1:]):
        total += term[pl.ds(start, rows)].astype(jnp.float32)
    out[...] = total.astype(jnp.bfloat16)


def stack_kernel(start, rows, *refs):
    *parts, out = refs
    for which, part in enumerate(parts):
        out[pl.ds(which * rows, rows)] = part[pl.ds(start, rows)]


class Device:
    def __init__(self, order, weights, mask):
        self.order, self.weights, self.mask = order, weights, mask

    def begin(self, chips, *sources):
        streams = sources[0]
        sent = jax.ShapeDtypeStruct((streams.shape[0] * streams.shape[1], streams.shape[2] + TAIL), jnp.bfloat16)
        sent, gate_w, up_w, down_w = self.order.call(
            functools.partial(begin_kernel, chips),
            [sent] + [pltpu.VMEM(w.shape, w.dtype) for w in self.weights],
            [ANYWHERE] * 7,
            [pltpu.with_memory_space_constraint(x, pltpu.HBM) for x in (*sources, *self.weights)],
            scratch_shapes=[pltpu.VMEM(x.shape, x.dtype) for x in sources] + [pltpu.SemaphoreType.DMA((7,))],
            name="begin",
        )
        self.weights = gate_w, up_w, down_w
        return sent

    def share(self):
        own = [self.order.wait(w) for w in self.weights]
        self.weights = (*own, *(swap_cores(w) for w in own))

    def ffn(self, blocks, parts):
        rows = sum(block.shape[0] for block in blocks) // parts
        return self.order.call(
            functools.partial(ffn_kernel, len(blocks)),
            [jax.ShapeDtypeStruct((rows, self.weights[0].shape[0]), jnp.bfloat16)] * parts,
            [NEAR] * (len(blocks) + 7),
            near(*blocks, self.mask, *self.weights),
            name="expert",
            compiler_params=pltpu.CompilerParams(vmem_limit_bytes=28 << 20),
        )

    def add(self, *terms, rows=None):
        terms = [term if isinstance(term, tuple) else (term, 0) for term in terms]
        rows = rows or terms[0][0].shape[0]
        return self.order.call(
            functools.partial(sum_kernel, [start for _, start in terms]),
            jax.ShapeDtypeStruct((rows, terms[0][0].shape[1]), jnp.bfloat16),
            [NEAR] * len(terms),
            near(*[term for term, _ in terms]),
            name="sum",
        )

    def stack(self, *parts, start, rows):
        return self.order.call(
            functools.partial(stack_kernel, start, rows),
            jax.ShapeDtypeStruct((len(parts) * rows, parts[0].shape[1]), jnp.bfloat16),
            [NEAR] * len(parts),
            near(*parts),
            name="stack",
        )


class Chunk:
    def __init__(self, device, own, state, local, pairs, together):
        self.device, self.own, self.state, self.local, self.pairs = device, own, state, local, pairs
        self.last = lax.axis_size("expert") // 2 - 2
        self.rows = own[0].shape[0] // 2
        self.together = together
        self.moving, self.held, self.partials, self.shifted = {}, {}, {}, []

    def depart(self, after=True):
        for part, own in enumerate(self.own):
            self.moving[part] = gather_hop(self.device.order.wait(own) if after else own, 0)

    def gather(self, step):
        blocks = []
        for part in range(len(self.own)):
            blocks.append(self.device.order.wait(self.moving[part]))
            if step < self.last:
                self.moving[part] = gather_hop(blocks[part], step + 1)
        self.held[step] = blocks

    def work(self, step):
        blocks = self.held.pop(step)
        self.partials[step] = self.device.ffn(blocks, 1 if self.together else len(blocks))

    def send_back(self):
        self.sums = [reduce_hop(partial, self.last) for partial in self.partials[self.last]]

    def go_on(self, step):
        for part, value in enumerate(self.sums):
            total = self.device.add(self.partials[step][part], self.device.order.wait(value))
            self.sums[part] = reduce_hop(total, step)

    def finish(self):
        rows = self.rows
        start = 0
        for value in self.sums:
            total = self.device.order.wait(value)
            cuts = range(0, total.shape[0], 2 * rows)
            theirs = swap_cores(jnp.concatenate([total[c + rows:c + 2 * rows] for c in cuts], axis=0))
            mine = jnp.concatenate([total[c:c + rows] for c in cuts], axis=0)
            state = self.state[start:start + mine.shape[0]]
            mixed = self.device.add(state, (self.local[0], self.local[1] + start), mine, theirs)
            self.shifted.append(lax.ppermute(mixed, "pipe", self.pairs))
            start += mine.shape[0]

    def settle(self):
        self.shifted = [self.device.order.wait(value) for value in self.shifted]

    def result(self):
        return jnp.concatenate(self.shifted, axis=0)


def body(streams, norm_gain, w_gate, w_up, w_down, routes, gate_weights):
    chips = lax.axis_size("expert") // 2
    sections = lax.axis_size("pipe")
    weights = (w_gate[0, 0], w_up[0, 0], w_down[0, 0])
    tokens = streams.shape[2]
    rows = tokens // PARTS
    lane = jnp.arange(TAIL)
    mask = ((lane % chips == lax.axis_index("expert") // 2) & (lane < 3 * chips)).astype(jnp.float32)[None]
    device = Device(Order(mask), weights, mask)
    sent = device.begin(
        chips, streams[0], norm_gain, routes[0].transpose(0, 2, 1), gate_weights[0].transpose(0, 2, 1)
    )
    swapped = swap_cores(sent)
    own = [
        [device.stack(sent, swapped, start=start, rows=rows) for start in range(first, first + tokens, rows)]
        for first in (0, tokens)
    ]
    chunks = []
    for stream in range(2):
        step = 1 if stream == 0 else sections - 1
        pairs = [(source, (source + step) % sections) for source in range(sections)]
        chunks.append(Chunk(device, own[stream], streams[0, stream], None, pairs, together=stream == 0))
    one, two = chunks
    last = one.last
    one.depart(after=False)
    device.share()
    for step in range(last):
        one.gather(step)
    two.depart()
    for step in range(last):
        one.work(step)
    one.gather(last)
    one.work(last)
    one.send_back()
    for step in range(last):
        two.gather(step)
        if step < last - 1:
            one.go_on(last - 1 - step)
    two.gather(last)
    two.work(last)
    two.send_back()
    one.go_on(0)
    for step in reversed(range(last)):
        two.work(step)
        if step == 0:
            (local,) = device.ffn([sent], 1)
            one.local, two.local = (local, 0), (local, tokens)
            one.finish()
        two.go_on(step)
    one.settle()
    two.finish()
    return jnp.stack([one.result(), two.result()])[None]


def solution(mesh):
    return jax.shard_map(
        body,
        mesh=mesh,
        in_specs=(
            P("pipe", None, "expert", None),
            P("pipe", None),
            P("pipe", "expert", None, None),
            P("pipe", "expert", None, None),
            P("pipe", "expert", None, None),
            P("pipe", None, "expert", None),
            P("pipe", None, "expert", None),
        ),
        out_specs=P("pipe", None, "expert", None),
        check_vma=False,
    )
```

```python
import functools

import jax
import jax.numpy as jnp
from jax import lax
from jax.experimental import pallas as pl
from jax.experimental.pallas import tpu as pltpu
from jax.sharding import PartitionSpec as P

PARTS = 2
TAIL = 128
NO_COST = pl.CostEstimate(flops=1024, bytes_accessed=1024, transcendentals=0)
NEAR = pl.BlockSpec(memory_space=pltpu.VMEM)
ANYWHERE = pl.BlockSpec(memory_space=pl.ANY)
LIMIT = pltpu.CompilerParams(vmem_limit_bytes=16 << 20)


def swap_cores(value):
    count = lax.axis_size("expert")
    return lax.ppermute(value, "expert", [(i, i ^ 1) for i in range(count)])


def hop_pairs(step):
    chips = lax.axis_size("expert") // 2
    up = [(2 * z, 2 * z + 2) for z in range(step, chips - 1)]
    down = [(2 * z + 1, 2 * z - 1) for z in range(1, chips - step)]
    return up + down


def gather_hop(value, step):
    return lax.ppermute(value, "expert", hop_pairs(step))


def reduce_hop(value, step):
    return lax.ppermute(value, "expert", [(target, source) for source, target in hop_pairs(step)])


def near(*values):
    return [pltpu.with_memory_space_constraint(x, pltpu.VMEM) for x in values]


class Order:
    def __init__(self, first):
        self.before = [first]

    def call(self, kernel, out_shape, in_specs, operands, out_specs=NEAR, **options):
        before, count = self.before, len(operands)
        result = pl.pallas_call(
            lambda *refs: kernel(*refs[:count], *refs[count + len(before):]),
            out_shape=out_shape,
            in_specs=in_specs + [ANYWHERE] * len(before),
            out_specs=jax.tree.map(lambda _: out_specs, out_shape),
            **{"compiler_params": LIMIT, "cost_estimate": NO_COST, **options},
        )(*operands, *before)
        self.before = [jax.tree.leaves(result)[0]]
        return result

    def wait(self, value):
        return self.call(
            lambda here, out: None,
            jax.ShapeDtypeStruct(value.shape, value.dtype),
            [ANYWHERE],
            [value],
            out_specs=ANYWHERE,
            input_output_aliases={0: 0},
            name="arrived",
        )


def load_kernel(up_in, down_in, up_out, down_out, sems):
    copies = [pltpu.make_async_copy(up_in, up_out, sems.at[0]), pltpu.make_async_copy(down_in, down_out, sems.at[1])]
    for copy in copies:
        copy.start()
    for copy in copies:
        copy.wait()


def begin_kernel(chips, *refs):
    sources, out, weight, copied, sems = refs[:5], refs[5], refs[6], refs[7:11], refs[11]
    copies = [pltpu.make_async_copy(a, b, sems.at[k]) for k, (a, b) in enumerate(zip(sources, (*copied, weight)))]
    for copy in copies:
        copy.start()
    for copy in copies[:4]:
        copy.wait()
    streams, gain, routes, gates = copied
    _, tokens, width = streams.shape
    square = (tokens, tokens)
    diagonal = lax.broadcasted_iota(jnp.int32, square, 0) == lax.broadcasted_iota(jnp.int32, square, 1)
    lane = lax.broadcasted_iota(jnp.int32, (tokens, TAIL), 1)
    expert, addend = jnp.full((tokens, TAIL), -1, jnp.int32), jnp.zeros((tokens, TAIL), jnp.int32)
    for which in range(3):
        for e in range(chips):
            here = lane == which * chips + e
            expert, addend = jnp.where(here, e, expert), jnp.where(here, which, addend)

    def column(row):
        return jnp.sum(jnp.where(diagonal, row, 0), axis=1, keepdims=True)

    for stream in range(streams.shape[0]):
        place = pl.ds(stream * tokens, tokens)
        state = streams[stream].astype(jnp.float32)
        scale = lax.rsqrt(jnp.mean(state * state, axis=-1, keepdims=True) + 1e-06)
        out[place, pl.ds(0, width)] = (state * scale * gain[...]).astype(jnp.bfloat16)
        left = jnp.zeros((tokens, TAIL), jnp.float32)
        for k in range(routes.shape[1]):
            named = column(routes[stream, pl.ds(k, 1)]) == expert
            left += jnp.where(named, column(gates[stream, pl.ds(k, 1)]), 0.0)
        tail = jnp.zeros((tokens, TAIL), jnp.float32)
        for which in range(3):
            rounded = left.astype(jnp.bfloat16).astype(jnp.float32)
            tail = jnp.where(addend == which, rounded, tail)
            left = left - rounded
        out[place, pl.ds(width, TAIL)] = tail.astype(jnp.bfloat16)
    for copy in copies[4:]:
        copy.wait()


def norm_kernel(chips, *refs):
    sources, outs, copied, sems = refs[:4], refs[4:-5], refs[-5:-1], refs[-1]
    copies = [pltpu.make_async_copy(a, b, sems.at[k]) for k, (a, b) in enumerate(zip(sources, copied))]
    for copy in copies:
        copy.start()
    for copy in copies:
        copy.wait()
    streams, gain, routes, gates = copied
    _, tokens, width = streams.shape
    square = (tokens, tokens)
    diagonal = lax.broadcasted_iota(jnp.int32, square, 0) == lax.broadcasted_iota(jnp.int32, square, 1)
    lane = lax.broadcasted_iota(jnp.int32, (tokens, TAIL), 1)
    expert, addend = jnp.full((tokens, TAIL), -1, jnp.int32), jnp.zeros((tokens, TAIL), jnp.int32)
    for which in range(3):
        for e in range(chips):
            here = lane == which * chips + e
            expert, addend = jnp.where(here, e, expert), jnp.where(here, which, addend)

    def column(row):
        return jnp.sum(jnp.where(diagonal, row, 0), axis=1, keepdims=True)

    for stream in range(streams.shape[0]):
        place = pl.ds(stream * tokens, tokens)
        state = streams[stream].astype(jnp.float32)
        scale = lax.rsqrt(jnp.mean(state * state, axis=-1, keepdims=True) + 1e-06)
        out[place, pl.ds(0, width)] = (state * scale * gain[...]).astype(jnp.bfloat16)
        left = jnp.zeros((tokens, TAIL), jnp.float32)
        for k in range(routes.shape[1]):
            named = column(routes[stream, pl.ds(k, 1)]) == expert
            left += jnp.where(named, column(gates[stream, pl.ds(k, 1)]), 0.0)
        tail = jnp.zeros((tokens, TAIL), jnp.float32)
        for which in range(3):
            rounded = left.astype(jnp.bfloat16).astype(jnp.float32)
            tail = jnp.where(addend == which, rounded, tail)
            left = left - rounded
        out[place, pl.ds(width, TAIL)] = tail.astype(jnp.bfloat16)
    for copy in copies[4:]:
        copy.wait()


def load_kernel(*refs):
    *pairs, sems = refs
    half = len(pairs) // 2
    copies = [pltpu.make_async_copy(pairs[k], pairs[half + k], sems.at[k]) for k in range(half)]
    for copy in copies:
        copy.start()
    for copy in copies:
        copy.wait()


def ffn_kernel(count, *refs):
    blocks, (mask, gate_a, up_a, down_a, gate_b, up_b, down_b), outs = refs[:count], refs[count:count + 7], refs[count + 7:]
    width = gate_a.shape[0]
    half = width // 2
    block = jnp.concatenate([b[...] for b in blocks], axis=0)
    rows = block[:, :width]
    scale = jnp.sum(block[:, width:].astype(jnp.float32) * mask[...], axis=-1, keepdims=True)

    def hidden(gate_w, up_w):
        gate_val = jnp.dot(rows, gate_w[...], preferred_element_type=jnp.float32)
        up_val = jnp.dot(rows, up_w[...], preferred_element_type=jnp.float32)
        return (gate_val / (1.0 + jnp.exp(-gate_val)) * up_val * scale).astype(jnp.bfloat16)

    first, second = hidden(gate_a, up_a), hidden(gate_b, up_b)
    for k in range(2):
        part = pl.ds(k * half, half)
        result = jnp.dot(first, down_a[:, part], preferred_element_type=jnp.float32)
        result += jnp.dot(second, down_b[:, part], preferred_element_type=jnp.float32)
        result = result.astype(jnp.bfloat16)
        start = 0
        for out in outs:
            out[:, part] = result[start:start + out.shape[0]]
            start += out.shape[0]


def sum_kernel(starts, *refs):
    *terms, out = refs
    rows = out.shape[0]
    total = terms[0][pl.ds(starts[0], rows)].astype(jnp.float32)
    for term, start in zip(terms[1:], starts[1:]):
        total += term[pl.ds(start, rows)].astype(jnp.float32)
    out[...] = total.astype(jnp.bfloat16)


def stack_kernel(start, rows, *refs):
    *parts, out = refs
    for which, part in enumerate(parts):
        out[pl.ds(which * rows, rows)] = part[pl.ds(start, rows)]


class Device:
    def __init__(self, order, weights, mask):
        self.order, self.weights, self.mask = order, weights, mask

    def begin(self, chips, *sources):
        streams = sources[0]
        sent = jax.ShapeDtypeStruct((streams.shape[0] * streams.shape[1], streams.shape[2] + TAIL), jnp.bfloat16)
        sent, gate_w = self.order.call(
            functools.partial(begin_kernel, chips),
            [sent] + [pltpu.VMEM(w.shape, w.dtype) for w in self.weights[:1]],
            [ANYWHERE] * 5,
            [pltpu.with_memory_space_constraint(x, pltpu.HBM) for x in (*sources, *self.weights[:1])],
            scratch_shapes=[pltpu.VMEM(x.shape, x.dtype) for x in sources] + [pltpu.SemaphoreType.DMA((5,))],
            name="begin",
        )
        up_w, down_w = self.order.call(
            load_kernel,
            [pltpu.VMEM(w.shape, w.dtype) for w in self.weights[1:]],
            [ANYWHERE] * 2,
            [pltpu.with_memory_space_constraint(x, pltpu.HBM) for x in self.weights[1:]],
            scratch_shapes=[pltpu.SemaphoreType.DMA((2,))],
            cost_estimate=pl.CostEstimate(flops=10**11, bytes_accessed=1024, transcendentals=0),
            name="load",
        )
        self.weights = gate_w, up_w, down_w
        return sent

    def share(self):
        own = [self.order.wait(w) for w in self.weights]
        self.weights = (*own, *(swap_cores(w) for w in own))

    def ffn(self, blocks, parts):
        rows = sum(block.shape[0] for block in blocks) // parts
        return self.order.call(
            functools.partial(ffn_kernel, len(blocks)),
            [jax.ShapeDtypeStruct((rows, self.weights[0].shape[0]), jnp.bfloat16)] * parts,
            [NEAR] * (len(blocks) + 7),
            near(*blocks, self.mask, *self.weights),
            name="expert",
            compiler_params=pltpu.CompilerParams(vmem_limit_bytes=28 << 20),
        )

    def add(self, *terms, rows=None):
        terms = [term if isinstance(term, tuple) else (term, 0) for term in terms]
        rows = rows or terms[0][0].shape[0]
        return self.order.call(
            functools.partial(sum_kernel, [start for _, start in terms]),
            jax.ShapeDtypeStruct((rows, terms[0][0].shape[1]), jnp.bfloat16),
            [NEAR] * len(terms),
            near(*[term for term, _ in terms]),
            name="sum",
        )

    def stack(self, *parts, start, rows):
        return self.order.call(
            functools.partial(stack_kernel, start, rows),
            jax.ShapeDtypeStruct((len(parts) * rows, parts[0].shape[1]), jnp.bfloat16),
            [NEAR] * len(parts),
            near(*parts),
            name="stack",
        )


class Chunk:
    def __init__(self, device, own, state, local, pairs, together):
        self.device, self.own, self.state, self.local, self.pairs = device, own, state, local, pairs
        self.last = lax.axis_size("expert") // 2 - 2
        self.rows = own[0].shape[0] // 2
        self.together = together
        self.moving, self.held, self.partials, self.shifted = {}, {}, {}, []

    def depart(self, after=True):
        for part, own in enumerate(self.own):
            self.moving[part] = gather_hop(self.device.order.wait(own) if after else own, 0)

    def gather(self, step):
        blocks = []
        for part in range(len(self.own)):
            blocks.append(self.device.order.wait(self.moving[part]))
            if step < self.last:
                self.moving[part] = gather_hop(blocks[part], step + 1)
        self.held[step] = blocks

    def work(self, step):
        blocks = self.held.pop(step)
        self.partials[step] = self.device.ffn(blocks, 1 if self.together else len(blocks))

    def send_back(self):
        self.sums = [reduce_hop(partial, self.last) for partial in self.partials[self.last]]

    def go_on(self, step):
        for part, value in enumerate(self.sums):
            total = self.device.add(self.partials[step][part], self.device.order.wait(value))
            self.sums[part] = reduce_hop(total, step)

    def finish(self):
        rows = self.rows
        start = 0
        for value in self.sums:
            total = self.device.order.wait(value)
            cuts = range(0, total.shape[0], 2 * rows)
            theirs = swap_cores(jnp.concatenate([total[c + rows:c + 2 * rows] for c in cuts], axis=0))
            mine = jnp.concatenate([total[c:c + rows] for c in cuts], axis=0)
            state = self.state[start:start + mine.shape[0]]
            mixed = self.device.add(state, (self.local[0], self.local[1] + start), mine, theirs)
            self.shifted.append(lax.ppermute(mixed, "pipe", self.pairs))
            start += mine.shape[0]

    def settle(self):
        self.shifted = [self.device.order.wait(value) for value in self.shifted]

    def result(self):
        return jnp.concatenate(self.shifted, axis=0)


def body(streams, norm_gain, w_gate, w_up, w_down, routes, gate_weights):
    chips = lax.axis_size("expert") // 2
    sections = lax.axis_size("pipe")
    weights = (w_gate[0, 0], w_up[0, 0], w_down[0, 0])
    tokens = streams.shape[2]
    rows = tokens // PARTS
    lane = jnp.arange(TAIL)
    mask = ((lane % chips == lax.axis_index("expert") // 2) & (lane < 3 * chips)).astype(jnp.float32)[None]
    device = Device(Order(mask), weights, mask)
    sent = device.begin(
        chips, streams[0], norm_gain, routes[0].transpose(0, 2, 1), gate_weights[0].transpose(0, 2, 1)
    )
    swapped = swap_cores(sent)
    own = [
        [device.stack(sent, swapped, start=start, rows=rows) for start in range(first, first + tokens, rows)]
        for first in (0, tokens)
    ]
    chunks = []
    for stream in range(2):
        step = 1 if stream == 0 else sections - 1
        pairs = [(source, (source + step) % sections) for source in range(sections)]
        chunks.append(Chunk(device, own[stream], streams[0, stream], None, pairs, together=stream == 0))
    one, two = chunks
    last = one.last
    one.depart(after=False)
    device.share()
    for step in range(last):
        one.gather(step)
    two.depart()
    for step in range(1, last):
        one.work(step)
    one.gather(last)
    one.work(last)
    one.send_back()
    for step in range(last):
        two.gather(step)
        if step == 0:
            one.work(0)
        if step < last - 1:
            one.go_on(last - 1 - step)
    two.gather(last)
    two.work(last)
    two.send_back()
    one.go_on(0)
    for step in reversed(range(last)):
        two.work(step)
        if step == 0:
            (local,) = device.ffn([sent], 1)
            one.local, two.local = (local, 0), (local, tokens)
            one.finish()
        two.go_on(step)
    one.settle()
    two.finish()
    return jnp.stack([one.result(), two.result()])[None]


def solution(mesh):
    return jax.shard_map(
        body,
        mesh=mesh,
        in_specs=(
            P("pipe", None, "expert", None),
            P("pipe", None),
            P("pipe", "expert", None, None),
            P("pipe", "expert", None, None),
            P("pipe", "expert", None, None),
            P("pipe", None, "expert", None),
            P("pipe", None, "expert", None),
        ),
        out_specs=P("pipe", None, "expert", None),
        check_vma=False,
    )
```

```python
import functools

import jax
import jax.numpy as jnp
from jax import lax
from jax.experimental import pallas as pl
from jax.experimental.pallas import tpu as pltpu
from jax.sharding import PartitionSpec as P

PARTS = 2
TAIL = 128
NO_COST = pl.CostEstimate(flops=1024, bytes_accessed=1024, transcendentals=0)
NEAR = pl.BlockSpec(memory_space=pltpu.VMEM)
ANYWHERE = pl.BlockSpec(memory_space=pl.ANY)
LIMIT = pltpu.CompilerParams(vmem_limit_bytes=16 << 20)


def swap_cores(value):
    count = lax.axis_size("expert")
    return lax.ppermute(value, "expert", [(i, i ^ 1) for i in range(count)])


def hop_pairs(step):
    chips = lax.axis_size("expert") // 2
    up = [(2 * z, 2 * z + 2) for z in range(step, chips - 1)]
    down = [(2 * z + 1, 2 * z - 1) for z in range(1, chips - step)]
    return up + down


def gather_hop(value, step):
    return lax.ppermute(value, "expert", hop_pairs(step))


def reduce_hop(value, step):
    return lax.ppermute(value, "expert", [(target, source) for source, target in hop_pairs(step)])


def near(*values):
    return [pltpu.with_memory_space_constraint(x, pltpu.VMEM) for x in values]


class Order:
    def __init__(self, first):
        self.before = [first]

    def call(self, kernel, out_shape, in_specs, operands, out_specs=NEAR, **options):
        before, count = self.before, len(operands)
        result = pl.pallas_call(
            lambda *refs: kernel(*refs[:count], *refs[count + len(before):]),
            out_shape=out_shape,
            in_specs=in_specs + [ANYWHERE] * len(before),
            out_specs=jax.tree.map(lambda _: out_specs, out_shape),
            **{"compiler_params": LIMIT, "cost_estimate": NO_COST, **options},
        )(*operands, *before)
        self.before = [jax.tree.leaves(result)[0]]
        return result

    def wait(self, value):
        return self.call(
            lambda here, out: None,
            jax.ShapeDtypeStruct(value.shape, value.dtype),
            [ANYWHERE],
            [value],
            out_specs=ANYWHERE,
            input_output_aliases={0: 0},
            name="arrived",
        )


def load_kernel(up_in, down_in, up_out, down_out, sems):
    copies = [pltpu.make_async_copy(up_in, up_out, sems.at[0]), pltpu.make_async_copy(down_in, down_out, sems.at[1])]
    for copy in copies:
        copy.start()
    for copy in copies:
        copy.wait()


def begin_kernel(chips, *refs):
    sources, out, weight, copied, sems = refs[:5], refs[5], refs[6], refs[7:11], refs[11]
    copies = [pltpu.make_async_copy(a, b, sems.at[k]) for k, (a, b) in enumerate(zip(sources, (*copied, weight)))]
    for copy in copies:
        copy.start()
    for copy in copies[:4]:
        copy.wait()
    streams, gain, routes, gates = copied
    _, tokens, width = streams.shape
    square = (tokens, tokens)
    diagonal = lax.broadcasted_iota(jnp.int32, square, 0) == lax.broadcasted_iota(jnp.int32, square, 1)
    lane = lax.broadcasted_iota(jnp.int32, (tokens, TAIL), 1)
    expert, addend = jnp.full((tokens, TAIL), -1, jnp.int32), jnp.zeros((tokens, TAIL), jnp.int32)
    for which in range(3):
        for e in range(chips):
            here = lane == which * chips + e
            expert, addend = jnp.where(here, e, expert), jnp.where(here, which, addend)

    def column(row):
        return jnp.sum(jnp.where(diagonal, row, 0), axis=1, keepdims=True)

    for stream in range(streams.shape[0]):
        place = pl.ds(stream * tokens, tokens)
        state = streams[stream].astype(jnp.float32)
        scale = lax.rsqrt(jnp.mean(state * state, axis=-1, keepdims=True) + 1e-06)
        out[place, pl.ds(0, width)] = (state * scale * gain[...]).astype(jnp.bfloat16)
        left = jnp.zeros((tokens, TAIL), jnp.float32)
        for k in range(routes.shape[1]):
            named = column(routes[stream, pl.ds(k, 1)]) == expert
            left += jnp.where(named, column(gates[stream, pl.ds(k, 1)]), 0.0)
        tail = jnp.zeros((tokens, TAIL), jnp.float32)
        for which in range(3):
            rounded = left.astype(jnp.bfloat16).astype(jnp.float32)
            tail = jnp.where(addend == which, rounded, tail)
            left = left - rounded
        out[place, pl.ds(width, TAIL)] = tail.astype(jnp.bfloat16)
    for copy in copies[4:]:
        copy.wait()


def norm_kernel(chips, *refs):
    sources, outs, copied, sems = refs[:4], refs[4:-5], refs[-5:-1], refs[-1]
    copies = [pltpu.make_async_copy(a, b, sems.at[k]) for k, (a, b) in enumerate(zip(sources, copied))]
    for copy in copies:
        copy.start()
    for copy in copies:
        copy.wait()
    streams, gain, routes, gates = copied
    _, tokens, width = streams.shape
    square = (tokens, tokens)
    diagonal = lax.broadcasted_iota(jnp.int32, square, 0) == lax.broadcasted_iota(jnp.int32, square, 1)
    lane = lax.broadcasted_iota(jnp.int32, (tokens, TAIL), 1)
    expert, addend = jnp.full((tokens, TAIL), -1, jnp.int32), jnp.zeros((tokens, TAIL), jnp.int32)
    for which in range(3):
        for e in range(chips):
            here = lane == which * chips + e
            expert, addend = jnp.where(here, e, expert), jnp.where(here, which, addend)

    def column(row):
        return jnp.sum(jnp.where(diagonal, row, 0), axis=1, keepdims=True)

    for stream in range(streams.shape[0]):
        place = pl.ds(stream * tokens, tokens)
        state = streams[stream].astype(jnp.float32)
        scale = lax.rsqrt(jnp.mean(state * state, axis=-1, keepdims=True) + 1e-06)
        out[place, pl.ds(0, width)] = (state * scale * gain[...]).astype(jnp.bfloat16)
        left = jnp.zeros((tokens, TAIL), jnp.float32)
        for k in range(routes.shape[1]):
            named = column(routes[stream, pl.ds(k, 1)]) == expert
            left += jnp.where(named, column(gates[stream, pl.ds(k, 1)]), 0.0)
        tail = jnp.zeros((tokens, TAIL), jnp.float32)
        for which in range(3):
            rounded = left.astype(jnp.bfloat16).astype(jnp.float32)
            tail = jnp.where(addend == which, rounded, tail)
            left = left - rounded
        out[place, pl.ds(width, TAIL)] = tail.astype(jnp.bfloat16)
    for copy in copies[4:]:
        copy.wait()


def load_kernel(*refs):
    *pairs, sems = refs
    half = len(pairs) // 2
    copies = [pltpu.make_async_copy(pairs[k], pairs[half + k], sems.at[k]) for k in range(half)]
    for copy in copies:
        copy.start()
    for copy in copies:
        copy.wait()


def ffn_kernel(count, *refs):
    blocks, (mask, gate_a, up_a, down_a, gate_b, up_b, down_b), outs = refs[:count], refs[count:count + 7], refs[count + 7:]
    width = gate_a.shape[0]
    half = width // 2
    block = jnp.concatenate([b[...] for b in blocks], axis=0)
    rows = block[:, :width]
    scale = jnp.sum(block[:, width:].astype(jnp.float32) * mask[...], axis=-1, keepdims=True)

    def hidden(gate_w, up_w):
        gate_val = jnp.dot(rows, gate_w[...], preferred_element_type=jnp.float32)
        up_val = jnp.dot(rows, up_w[...], preferred_element_type=jnp.float32)
        return (gate_val / (1.0 + jnp.exp(-gate_val)) * up_val * scale).astype(jnp.bfloat16)

    first, second = hidden(gate_a, up_a), hidden(gate_b, up_b)
    for k in range(2):
        part = pl.ds(k * half, half)
        result = jnp.dot(first, down_a[:, part], preferred_element_type=jnp.float32)
        result += jnp.dot(second, down_b[:, part], preferred_element_type=jnp.float32)
        result = result.astype(jnp.bfloat16)
        start = 0
        for out in outs:
            out[:, part] = result[start:start + out.shape[0]]
            start += out.shape[0]


def sum_kernel(starts, *refs):
    *terms, out = refs
    rows = out.shape[0]
    total = terms[0][pl.ds(starts[0], rows)].astype(jnp.float32)
    for term, start in zip(terms[1:], starts[1:]):
        total += term[pl.ds(start, rows)].astype(jnp.float32)
    out[...] = total.astype(jnp.bfloat16)


def stack_kernel(start, rows, *refs):
    *parts, out = refs
    for which, part in enumerate(parts):
        out[pl.ds(which * rows, rows)] = part[pl.ds(start, rows)]


class Device:
    def __init__(self, order, weights, mask):
        self.order, self.weights, self.mask = order, weights, mask

    def begin(self, chips, *sources):
        streams = sources[0]
        sent = jax.ShapeDtypeStruct((streams.shape[0] * streams.shape[1], streams.shape[2] + TAIL), jnp.bfloat16)
        sent, gate_w = self.order.call(
            functools.partial(begin_kernel, chips),
            [sent] + [pltpu.VMEM(w.shape, w.dtype) for w in self.weights[:1]],
            [ANYWHERE] * 5,
            [pltpu.with_memory_space_constraint(x, pltpu.HBM) for x in (*sources, *self.weights[:1])],
            scratch_shapes=[pltpu.VMEM(x.shape, x.dtype) for x in sources] + [pltpu.SemaphoreType.DMA((5,))],
            name="begin",
        )
        up_w, down_w = self.order.call(
            load_kernel,
            [pltpu.VMEM(w.shape, w.dtype) for w in self.weights[1:]],
            [ANYWHERE] * 2,
            [pltpu.with_memory_space_constraint(x, pltpu.HBM) for x in self.weights[1:]],
            scratch_shapes=[pltpu.SemaphoreType.DMA((2,))],
            cost_estimate=pl.CostEstimate(flops=10**11, bytes_accessed=1024, transcendentals=0),
            name="load",
        )
        self.weights = gate_w, up_w, down_w
        return sent

    def share(self):
        own = [self.order.wait(w) for w in self.weights]
        self.weights = (*own, *(swap_cores(w) for w in own))

    def ffn(self, blocks, parts):
        rows = sum(block.shape[0] for block in blocks) // parts
        return self.order.call(
            functools.partial(ffn_kernel, len(blocks)),
            [jax.ShapeDtypeStruct((rows, self.weights[0].shape[0]), jnp.bfloat16)] * parts,
            [NEAR] * (len(blocks) + 7),
            near(*blocks, self.mask, *self.weights),
            name="expert",
            compiler_params=pltpu.CompilerParams(vmem_limit_bytes=28 << 20),
        )

    def add(self, *terms, rows=None):
        terms = [term if isinstance(term, tuple) else (term, 0) for term in terms]
        rows = rows or terms[0][0].shape[0]
        return self.order.call(
            functools.partial(sum_kernel, [start for _, start in terms]),
            jax.ShapeDtypeStruct((rows, terms[0][0].shape[1]), jnp.bfloat16),
            [NEAR] * len(terms),
            near(*[term for term, _ in terms]),
            name="sum",
        )

    def stack(self, *parts, start, rows):
        return self.order.call(
            functools.partial(stack_kernel, start, rows),
            jax.ShapeDtypeStruct((len(parts) * rows, parts[0].shape[1]), jnp.bfloat16),
            [NEAR] * len(parts),
            near(*parts),
            name="stack",
        )


class Chunk:
    def __init__(self, device, own, state, local, pairs, together):
        self.device, self.own, self.state, self.local, self.pairs = device, own, state, local, pairs
        self.last = lax.axis_size("expert") // 2 - 2
        self.rows = own[0].shape[0] // 2
        self.together = together
        self.moving, self.held, self.partials, self.shifted = {}, {}, {}, []

    def depart(self, after=True):
        for part, own in enumerate(self.own):
            self.moving[part] = gather_hop(self.device.order.wait(own) if after else own, 0)

    def gather(self, step):
        blocks = []
        for part in range(len(self.own)):
            blocks.append(self.device.order.wait(self.moving[part]))
            if step < self.last:
                self.moving[part] = gather_hop(blocks[part], step + 1)
        self.held[step] = blocks

    def work(self, step):
        blocks = self.held.pop(step)
        self.partials[step] = self.device.ffn(blocks, 1 if self.together else len(blocks))

    def send_back(self):
        self.sums = [reduce_hop(partial, self.last) for partial in self.partials[self.last]]

    def go_on(self, step):
        for part, value in enumerate(self.sums):
            total = self.device.add(self.partials[step][part], self.device.order.wait(value))
            self.sums[part] = reduce_hop(total, step)

    def finish(self):
        rows = self.rows
        start = 0
        for value in self.sums:
            total = self.device.order.wait(value)
            cuts = range(0, total.shape[0], 2 * rows)
            theirs = swap_cores(jnp.concatenate([total[c + rows:c + 2 * rows] for c in cuts], axis=0))
            mine = jnp.concatenate([total[c:c + rows] for c in cuts], axis=0)
            state = self.state[start:start + mine.shape[0]]
            mixed = self.device.add(state, (self.local[0], self.local[1] + start), mine, theirs)
            self.shifted.append(lax.ppermute(mixed, "pipe", self.pairs))
            start += mine.shape[0]

    def settle(self):
        self.shifted = [self.device.order.wait(value) for value in self.shifted]

    def result(self):
        return jnp.concatenate(self.shifted, axis=0)


def body(streams, norm_gain, w_gate, w_up, w_down, routes, gate_weights):
    chips = lax.axis_size("expert") // 2
    sections = lax.axis_size("pipe")
    weights = (w_gate[0, 0], w_up[0, 0], w_down[0, 0])
    tokens = streams.shape[2]
    rows = tokens // PARTS
    lane = jnp.arange(TAIL)
    mask = ((lane % chips == lax.axis_index("expert") // 2) & (lane < 3 * chips)).astype(jnp.float32)[None]
    device = Device(Order(mask), weights, mask)
    sent = device.begin(
        chips, streams[0], norm_gain, routes[0].transpose(0, 2, 1), gate_weights[0].transpose(0, 2, 1)
    )
    swapped = swap_cores(sent)
    own = [
        [device.stack(sent, swapped, start=start, rows=rows) for start in range(first, first + tokens, rows)]
        for first in (0, tokens)
    ]
    chunks = []
    for stream in range(2):
        step = 1 if stream == 0 else sections - 1
        pairs = [(source, (source + step) % sections) for source in range(sections)]
        chunks.append(Chunk(device, own[stream], streams[0, stream], None, pairs, together=stream == 0))
    one, two = chunks
    last = one.last
    one.depart(after=False)
    device.share()
    for step in range(last):
        one.gather(step)
    two.depart()
    for step in range(1, last):
        one.work(step)
    one.gather(last)
    one.work(last)
    one.send_back()
    two.gather(0)
    one.work(0)
    for step in range(1, last + 1):
        two.gather(step)
        if step < last:
            one.go_on(last - step)
    two.work(last)
    two.send_back()
    one.go_on(0)
    for step in reversed(range(last)):
        two.work(step)
        if step == 0:
            (local,) = device.ffn([sent], 1)
            one.local, two.local = (local, 0), (local, tokens)
            one.finish()
        two.go_on(step)
    one.settle()
    two.finish()
    return jnp.stack([one.result(), two.result()])[None]


def solution(mesh):
    return jax.shard_map(
        body,
        mesh=mesh,
        in_specs=(
            P("pipe", None, "expert", None),
            P("pipe", None),
            P("pipe", "expert", None, None),
            P("pipe", "expert", None, None),
            P("pipe", "expert", None, None),
            P("pipe", None, "expert", None),
            P("pipe", None, "expert", None),
        ),
        out_specs=P("pipe", None, "expert", None),
        check_vma=False,
    )
```
